128 devices in a mesh: row: 8 (over y, core), col: 16 (over x, z).
Axes of the slice: x: 4, y: 4, z: 4, core: 2. Of those that a mesh axis runs over, the one named last changes fastest.
Arguments:
- table: float32 [512, 524288], P('col', 'row'), may hold values from -6 to 6
- accum: float32 [524288], P('row'), may hold values from 0.05 to 1
- grad_pooled: float32 [512, 16384], P('col', 'row')
- bag_of: int32 [8, 32768], P('row'), may hold values from 0 to 2047, never falling along the last dimension, each value on 1 to 64 neighbouring positions
- slots: int32 [8, 32768], P('row'), may hold values from 0 to 16383
- dirty_rows: int32 [8, 16384], P('row'), may hold values from 0 to 65535, as said below
- owner: int32 [131072, 1], P('row'), may hold values from 0 to 7; in each aligned block of 1024 rows (0 to 1023, 1024 to 2047, ...) at most 256 rows name the same one
Outputs:
- owned_rows: float32 [512, 262144], P(None, ('row', 'col'))
- accum_dirty: float32 [131072], P(('row', 'col'))
The draws below stay inside these ranges and needn't reach their ends.
Inputs may be any that keep to these rules, and one draw needn't show every extreme that they name: `dirty_rows`: within one row shard the slots name distinct cached rows. Within each aligned block of 1024 slots no owner is named more than 256 times. `bag_of`: never falling along a shard's entries; every bag has at least one entry.
All inputs are finite; a program needn't handle non-finite values.
Results may differ from the reference program's by a relative error of at most 0.0003.
Values sent between devices are 32-bit elements; how exact they have to be, the bound alone decides.
No kernel may reach another device: no remote copies, remote signals or barrier semaphores. Data moves between devices by JAX's collectives and lax.ppermute only.
A program may use at most 192 MiB of HBM per device.

```python
import math
import jax
import jax.numpy as jnp
import numpy as np
from jax import lax

WIDTH = 512
CACHE_DEV = 65536
FWD_DEV = 1024
BAGS_DEV = 2048
POOL = 16
ENTRY_DEV = 32768
DIRTY_DEV = 16384
CAP = 256
DIRTY = 131072
CACHE = 524288
N_ROW = 8
N_COL = 16


def draw_grad_pooled(key, part):
    key = jax.random.fold_in(key, 11)
    keys = jax.random.split(key, 3)
    columns = BAGS_DEV * N_ROW
    ramp = jnp.exp(math.log(3.0) * jnp.arange(WIDTH, dtype=jnp.float32) / (WIDTH - 1))
    jitter = jnp.exp(jax.random.uniform(keys[0], (WIDTH,), jnp.float32, 0.0, math.log(3.3)))
    bag_scale = jnp.exp(jax.random.uniform(keys[1], (1, columns), jnp.float32, 0.0, math.log(10.0)))
    base = jax.random.normal(keys[2], (WIDTH, columns), jnp.float32)
    factor = 0.3
    return factor * (ramp * jitter)[:, None] * bag_scale * base


def draw_dirty_rows(key, part):
    key = jax.random.fold_in(key, 5)

    def shard_list(shard_key):
        first_key, second_key = jax.random.split(shard_key)
        shuffled = jax.random.permutation(first_key, CACHE_DEV).astype(jnp.int32)
        chosen_spot = jax.random.randint(second_key, (), 0, DIRTY_DEV)
        top_place = jnp.argmax(shuffled == CACHE_DEV - 1)
        displaced = shuffled[chosen_spot]
        shuffled = shuffled.at[top_place].set(displaced).at[chosen_spot].set(CACHE_DEV - 1)
        return shuffled[:DIRTY_DEV]
    return jax.vmap(shard_list)(jax.random.split(key, N_ROW)).astype(jnp.int32)


def touch_ends(result, key, least, top_value):
    dims = result.shape
    place = [jax.random.randint(jax.random.fold_in(key, axis), (), 0, dims[axis]) for axis in range(len(dims))]
    result = result.at[tuple(place)].set(least)
    longest = dims.index(max(dims))
    place[longest] = (place[longest] + 1) % dims[longest]
    return result.at[tuple(place)].set(top_value)


def levels(key, dims, shards, smallest, largest):
    def one(axis_at, parts):
        draws = jax.random.uniform(jax.random.fold_in(jax.random.fold_in(key, 6), axis_at), (parts,), jnp.float32, smallest / len(shards), largest / len(shards))
        return jnp.repeat(jnp.exp(draws), dims[axis_at] // parts).reshape((-1,) + (1,) * (len(dims) - axis_at - 1))

    loudness = one(*shards[0])
    for cut in shards[1:]:
        loudness = loudness * one(*cut)
    return loudness


def cumulative_ranks(number_of, lean):
    loads = [(1 << 20) // math.isqrt(standing ** lean) + 1 for standing in range(1, number_of + 1)]
    deviation = 1 + sum(loads) // (1 << 30)
    return np.cumsum(np.array([max(1, weight // deviation) for weight in loads]))


def ranked(key, dims, number_of, skew):
    listing = cumulative_ranks(number_of, skew)
    ticket = jax.random.randint(jax.random.fold_in(key, 1), dims, 0, int(listing[number_of - 1]))
    rank = jnp.searchsorted(jnp.asarray(listing, jnp.int32), ticket, side="right")
    return jax.random.permutation(jax.random.fold_in(key, 2), number_of)[rank].astype(jnp.int32)


def length_profile(amount, total, bound, skew):
    loads = [(1 << 20) // math.isqrt(grade ** skew) + 1 for grade in range(2, amount + 1)]
    spare, given = total - bound - (amount - 1), [1] * (amount - 1)
    while spare > 0:
        candidates = [i for i in range(amount - 1) if given[i] < bound]
        mass, left = sum([loads[i] for i in candidates]), spare
        for i in candidates:
            addition = min(bound - given[i], max(1, left * loads[i] // mass), spare)
            given[i] = given[i] + addition
            spare = spare - addition
    return np.array([bound] + given)


def uneven(rng, amount, total, limit, slope):
    if amount == 2:
        one = jax.random.randint(rng, (), max(1, total - limit), min(limit, total - 1) + 1)
        return jnp.stack([one, total - one])
    sizes = jnp.asarray(length_profile(amount, total, limit, slope), jnp.int32)
    twos = (amount - 1) // 2
    giver, taker = sizes[1:1 + 2 * twos:2], sizes[2:2 + 2 * twos:2]
    room = jnp.minimum(giver - 1, limit - taker)
    moved = jax.random.randint(jax.random.fold_in(rng, 1), (twos,), 0, 1 << 20) % (room + 1)
    sizes = sizes.at[1:1 + 2 * twos:2].set(giver - moved).at[2:2 + 2 * twos:2].set(taker + moved)
    return sizes[jax.random.permutation(jax.random.fold_in(rng, 2), amount)]


def assign_block(stream_key, own, number, rows, count, top, reach, slope):
    sequence = jax.random.permutation(stream_key, count)
    heavy_load, ordinary = load_shares(count, rows * top, reach, slope, True), load_shares(count, rows * top, reach, slope, False)
    places = jnp.arange(count)

    def named(sizes, turn):
        used = int((sizes > 0).sum())
        fixed = max(1, used // 4)
        passed = fixed + (places - fixed + turn * (used - fixed)) % max(1, count - fixed)
        return jnp.zeros((count,), jnp.int32).at[sequence[jnp.where(places < fixed, places, passed)]].set(jnp.asarray(sizes, jnp.int32))

    sizes = jnp.where(number % 4 == 0, named(heavy_load, number // 4), named(ordinary, number - number // 4 - 1))
    mixed = jax.random.permutation(jax.random.fold_in(own, 3), count)
    donor, sink = mixed[0:count // 2 * 2:2], mixed[1:count // 2 * 2:2]
    slack = jnp.minimum(sizes[donor] - 1, reach - sizes[sink]) // 2
    slack = jnp.where((donor == sequence[0]) | (sink == sequence[0]) | (sizes[sink] == 0), 0, jnp.maximum(slack, 0))
    passed = jax.random.randint(jax.random.fold_in(own, 4), (count // 2,), 0, 1 << 20) % (slack + 1)
    sizes = sizes.at[donor].add(-passed).at[sink].add(passed)
    labels = jnp.searchsorted(jnp.cumsum(sizes), jnp.arange(rows * top), side="right").astype(jnp.int32)
    listing = labels.reshape(top, rows).T
    listing = listing[jax.random.permutation(jax.random.fold_in(own, 1), rows)]
    turn = jax.random.randint(jax.random.fold_in(own, 2), (rows, 1), 0, top)
    return jnp.take_along_axis(listing, (jnp.arange(top)[None, :] + turn) % top, axis=1)


def load_shares(count, total, limit, slope, full):
    loads = [(1 << 20) // math.isqrt(rank ** slope) + 1 for rank in range(1, count + 1)]
    largest = limit if full else min(limit, max(-(-total // count), total * loads[0] // sum(loads)))
    least = 1 if total - largest >= count - 1 else 0
    given, spare = [largest] + [least] * (count - 1), total - largest - least * (count - 1)
    while spare > 0:
        free = [i for i in range(1, count) if given[i] < largest] or [i for i in range(1, count) if given[i] < limit]
        mass, left = sum([loads[i] for i in free]), spare
        for i in free:
            more = min(limit - given[i], max(1, left * loads[i] // mass), spare)
            given[i] = given[i] + more
            spare = spare - more
    return np.array(given)


def gaussian(own_key, extent, width, bound, cuts=(), held_as=jnp.bfloat16):
    values = jax.random.normal(own_key, extent, jnp.float32) * width
    if len(cuts) > 0:
        values = levels(own_key, extent, cuts, -0.22, 0.18) * values
    return jnp.clip(values, min=-bound, max=bound).astype(held_as)


def setup_inputs(seed: int = 0) -> dict:
    arg_keys = jax.random.split(jax.random.key(seed), 8)
    table = gaussian(arg_keys[0], (WIDTH, CACHE), 1.0, 6.0, ((0, 16), (1, 8)), jnp.float32)
    accum = jnp.clip(jnp.exp(math.log(1.0) - 2.9957323 * jax.random.uniform(arg_keys[1], (CACHE,), jnp.float32) ** levels(arg_keys[1], (CACHE,), ((0, 8),), -0.2, 0.2)), 0.05, 1.0)
    grad_pooled = draw_grad_pooled(jax.random.fold_in(arg_keys[7], 71), 0)
    bag_of = jax.vmap(lambda own: jnp.searchsorted(jnp.cumsum(uneven(own, BAGS_DEV, ENTRY_DEV, 4 * POOL, 2)), jnp.arange(ENTRY_DEV), side="right"))(jax.random.split(arg_keys[3], N_ROW)).reshape((N_ROW, ENTRY_DEV)).astype(jnp.int32)
    slots = touch_ends(ranked(arg_keys[4], (N_ROW, ENTRY_DEV), DIRTY_DEV, 2), jax.random.fold_in(arg_keys[4], 3), 0, DIRTY_DEV - 1).astype(jnp.int32)
    dirty_rows = draw_dirty_rows(jax.random.fold_in(arg_keys[7], 71), 0)
    owner_keys = jax.random.split(jax.random.fold_in(arg_keys[6], 1), DIRTY // FWD_DEV)
    owner_turns = jax.random.permutation(jax.random.fold_in(arg_keys[6], 3), DIRTY // FWD_DEV)
    owner = jax.vmap(lambda own, number: assign_block(jax.random.fold_in(arg_keys[6], 2), own, number, FWD_DEV, N_ROW, 1, CAP, 2))(owner_keys, owner_turns).reshape((DIRTY, 1))
    return {"table": table, "accum": accum, "grad_pooled": grad_pooled, "bag_of": bag_of, "slots": slots, "dirty_rows": dirty_rows, "owner": owner}


learn_rate = 0.3
epsilon = 1e-08

def slot_places(owner_grid, owner_count):
    onehot = (owner_grid[..., None] == jnp.arange(owner_count, dtype=jnp.int32)).astype(jnp.int32)
    earlier = jnp.cumsum(onehot, axis=-2) - onehot
    return lax.optimization_barrier(jnp.sum(earlier * onehot, axis=-1)).astype(jnp.int32)

def reference(table, accum, grad_pooled, bag_of, slots, dirty_rows, owner):

    def per_shard(shard_index):
        bag_ids = bag_of[shard_index] + shard_index * BAGS_DEV
        entry_grad = jnp.take(grad_pooled, bag_ids, axis=1)
        row_grads = jnp.zeros((WIDTH, DIRTY_DEV), jnp.float32).at[:, slots[shard_index]].add(entry_grad)
        row_ids = dirty_rows[shard_index] + shard_index * CACHE_DEV
        old_rows = jnp.take(table, row_ids, axis=1)
        accum_new = accum[row_ids] + lax.optimization_barrier(jnp.sum(row_grads * row_grads, axis=0)) / WIDTH
        updated = old_rows - learn_rate * row_grads / (jnp.sqrt(accum_new) + epsilon)
        return (updated, accum_new)
    updated, accum_new = lax.map(per_shard, jnp.arange(N_ROW, dtype=jnp.int32))
    updated = jnp.transpose(updated, (1, 0, 2)).reshape(WIDTH, DIRTY)
    owner_grid = owner[:, 0].reshape(N_ROW, N_COL, FWD_DEV)
    places = slot_places(owner_grid, N_ROW)
    col_ids = jnp.arange(N_COL, dtype=jnp.int32)[None, :, None]
    shard_ids = jnp.arange(N_ROW, dtype=jnp.int32)[:, None, None]
    target = (((owner_grid * N_COL + col_ids) * N_ROW + shard_ids) * CAP + places).reshape(-1)
    owned_rows = jnp.zeros((WIDTH, N_ROW * N_COL * N_ROW * CAP), jnp.float32).at[:, target].set(updated)
    return (owned_rows, accum_new.reshape(-1))
```

```python
import jax
import jax.numpy as jnp
from jax import lax
from jax.experimental import pallas as pl
from jax.experimental.pallas import tpu as pltpu
from jax.sharding import PartitionSpec as P

learn_rate = 0.3
epsilon = 1e-08

LANES = 128
CAP = 256
CHUNK = 512
BAGS = 64
LOW = 256
VMEM_LIMIT = 48 * 1024 * 1024

f32, bf16, i32 = jnp.float32, jnp.bfloat16, jnp.int32
NT = (((1,), (1,)), ((), ()))
NN = (((1,), (0,)), ((), ()))


def split(x):
    high = x.astype(bf16)
    return high, (x - high.astype(f32)).astype(bf16)


def params(limit=VMEM_LIMIT):
    return pltpu.CompilerParams(vmem_limit_bytes=limit)


def plan_body(row_ref, row_col_ref, own_ref, own_col_ref, accum_ref, srt_ref, tgt_ref, tgt_srt_ref, acc_ref):
    n = row_ref.shape[1]
    step = 256
    row, own = row_ref[...], own_ref[...]
    place = jnp.zeros((1, n), i32)
    srt = jnp.zeros((1, n), i32)
    tgt_srt = jnp.zeros((1, n), i32)
    lane = lax.broadcasted_iota(i32, (step, n), 1)
    for i in range(0, n, step):
        rows = row_col_ref[i : i + step, :]
        owns = own_col_ref[i : i + step, :]
        at = lax.broadcasted_iota(i32, (step, n), 0) + i
        rank = jnp.sum(jnp.where(row < rows, 1.0, 0.0), axis=1, keepdims=True).astype(i32)
        same = own == owns
        places = jnp.sum(
            jnp.where(same & (lane < at), 1.0, 0.0), axis=1, keepdims=True
        ).astype(i32)
        hit = rank == lane
        srt = srt + jnp.sum(jnp.where(hit, rows, 0), axis=0, keepdims=True)
        tgt_srt = tgt_srt + jnp.sum(
            jnp.where(hit, owns * CAP + places, 0), axis=0, keepdims=True
        )
        place = place + jnp.sum(jnp.where(same & (at < lane), 1, 0), axis=0, keepdims=True)
    srt_ref[...] = srt
    tgt_srt_ref[...] = tgt_srt
    tgt_ref[...] = own * CAP + place
    tall = accum_ref.shape[1]
    picker = jnp.where(
        lax.broadcasted_iota(i32, (tall, n), 0) == row // LANES, 1.0, 0.0
    )
    wide = lax.dot_general(
        accum_ref[...], picker, NN, precision=lax.Precision.HIGHEST, preferred_element_type=f32
    )
    keep = lax.broadcasted_iota(i32, (LANES, n), 0) == row % LANES
    acc_ref[...] = jnp.sum(jnp.where(keep, wide, 0.0), axis=0, keepdims=True)


def plan(rows, owners, accum):
    n = rows.shape[0]
    out = jax.ShapeDtypeStruct((1, n), i32)
    return pl.pallas_call(
        plan_body,
        out_shape=(out, out, out, jax.ShapeDtypeStruct((1, n), f32)),
        compiler_params=params(),
        name="plan",
    )(
        rows[None, :],
        rows[:, None],
        owners[None, :],
        owners[:, None],
        accum.reshape(-1, LANES).T,
    )


def counts_body(first_ref, last_ref, block_ref, bag_ref, slot_ref, out_ref):
    highs, bags, low = out_ref.shape
    span = highs * low
    rows = highs * BAGS
    chunks, chunk = bag_ref.shape

    def clear(i, carry):
        for h in range(highs):
            out_ref[h, pl.ds(pl.multiple_of(i * BAGS, BAGS), BAGS), :] = jnp.zeros(
                (BAGS, low), bf16
            )
        return carry

    lax.fori_loop(0, bags // BAGS, clear, 0)
    start = block_ref[0] * span
    left_iota = lax.broadcasted_iota(i32, (rows, chunk), 0)
    right_iota = lax.broadcasted_iota(i32, (low, chunk), 0)

    def one_chunk(i, carry):
        slot = slot_ref[pl.ds(i, 1), :] - start
        bag = bag_ref[pl.ds(i, 1), :]
        inside = (slot >= 0) & (slot < span)
        right = jnp.where(right_iota == (slot & (low - 1)), 1.0, 0.0).astype(bf16)
        base = jnp.where(inside, (slot // low) * BAGS, -(1 << 20))

        def one_window(w, carry):
            near = bag - w * BAGS
            left_id = jnp.where((near >= 0) & (near < BAGS), base + near, -1)
            left = jnp.where(left_iota == left_id, 1.0, 0.0).astype(bf16)
            both = lax.dot_general(left, right, NT, preferred_element_type=f32)
            at = pl.ds(pl.multiple_of(w * BAGS, BAGS), BAGS)
            for h in range(highs):
                piece = both[h * BAGS : (h + 1) * BAGS].astype(bf16)
                out_ref[h, at, :] = out_ref[h, at, :] + piece
            return carry

        return lax.fori_loop(first_ref[i], last_ref[i] + 1, one_window, carry)

    lax.fori_loop(0, chunks, one_chunk, 0)


def pair_counts(bag_of, slots, block, bags, span):
    chunks = bag_of.shape[0] // CHUNK
    bag = bag_of.reshape(chunks, CHUNK)
    smem = pl.BlockSpec(memory_space=pltpu.SMEM)
    vmem = pl.BlockSpec(memory_space=pltpu.VMEM)
    return pl.pallas_call(
        counts_body,
        out_shape=jax.ShapeDtypeStruct((span // LOW, bags, LOW), bf16),
        in_specs=[smem, smem, smem, vmem, vmem],
        out_specs=vmem,
        compiler_params=params(),
        cost_estimate=pl.CostEstimate(flops=int(8e9), bytes_accessed=5 << 20, transcendentals=0),
        name="pair_counts",
    )(
        bag[:, 0] // BAGS,
        bag[:, CHUNK - 1] // BAGS,
        block[None],
        bag,
        slots.reshape(chunks, CHUNK),
    )


UNROLL = 8


def gather_body(first_ref, last_ref, srt_ref, table_ref, out_ref):
    width, columns = table_ref.shape
    tiles = srt_ref.shape[1]
    groups = width // 8
    top = columns // LANES - 1
    block = pl.program_id(0)

    for t in range(tiles):
        row = srt_ref[0, t : t + 1, :]
        lane = jnp.broadcast_to(row % LANES, (8, LANES))
        tile = jnp.broadcast_to(row // LANES, (8, LANES))
        first = first_ref[block, t]
        steps = (last_ref[block, t] - first) // UNROLL + 1

        def step(i, accs):
            accs = list(accs)
            for u in range(UNROLL):
                v = jnp.minimum(first + i * UNROLL + u, top)
                at = pl.ds(pl.multiple_of(v * LANES, LANES), LANES)
                here = tile == v
                for g in range(groups):
                    part = table_ref[g * 8 : (g + 1) * 8, at]
                    picked = jnp.take_along_axis(part, lane, axis=1, mode="promise_in_bounds")
                    accs[g] = jnp.where(here, picked, accs[g])
            return tuple(accs)

        zero = jnp.zeros((8, LANES), f32)
        accs = lax.fori_loop(0, steps, step, (zero,) * groups)
        for g in range(groups):
            out_ref[0, g * 8 : (g + 1) * 8, t * LANES : (t + 1) * LANES] = accs[g]


def gather_rows(table, srt):
    width = table.shape[0]
    blocks, n = srt.shape
    tiles = n // LANES
    srt = srt.reshape(blocks, tiles, LANES)
    return pl.pallas_call(
        gather_body,
        grid_spec=pltpu.PrefetchScalarGridSpec(
            num_scalar_prefetch=2,
            grid=(blocks,),
            in_specs=[
                pl.BlockSpec((1, tiles, LANES), lambda b, *_: (b, 0, 0)),
                pl.BlockSpec(table.shape, lambda b, *_: (0, 0)),
            ],
            out_specs=pl.BlockSpec((1, width, n), lambda b, *_: (b, 0, 0)),
        ),
        out_shape=jax.ShapeDtypeStruct((blocks, width, n), f32),
        compiler_params=params(),
        cost_estimate=pl.CostEstimate(flops=int(1e9), bytes_accessed=10 << 20, transcendentals=0),
        name="gather_rows",
    )(srt[:, :, 0] // LANES, srt[:, :, LANES - 1] // LANES, srt, table)


def step_body(grad_ref, count_ref, old_ref, step_ref, new_ref, high_ref, low_ref):
    width = grad_ref.shape[0]
    tile = 128

    @pl.when(pl.program_id(0) == 0)
    def _():
        def cut(i, carry):
            at = pl.ds(pl.multiple_of(i * 32, 32), 32)
            high_ref[at, :], low_ref[at, :] = split(grad_ref[at, :])
            return carry

        lax.fori_loop(0, width // 32, cut, 0)

    count = count_ref[0]

    def one(i, total):
        at = pl.ds(pl.multiple_of(i * tile, tile), tile)
        grads = lax.dot_general(high_ref[at, :], count, NN, preferred_element_type=f32)
        grads = grads + lax.dot_general(low_ref[at, :], count, NN, preferred_element_type=f32)
        step_ref[at, :] = grads
        return total + jnp.sum(grads * grads, axis=0, keepdims=True)

    low = count.shape[1]
    total = lax.fori_loop(0, width // tile, one, jnp.zeros((1, low), f32))
    new = old_ref[...] + total / width
    new_ref[...] = new
    factor = learn_rate / (jnp.sqrt(new) + epsilon)
    step_ref[...] = step_ref[...] * factor


def steps_of(grad, count, old):
    width, bags = grad.shape
    highs, _, low = count.shape
    return pl.pallas_call(
        step_body,
        grid=(highs,),
        in_specs=[
            pl.BlockSpec((width, bags), lambda h: (0, 0)),
            pl.BlockSpec((1, bags, low), lambda h: (h, 0, 0)),
            pl.BlockSpec((1, low), lambda h: (0, h)),
        ],
        out_specs=[
            pl.BlockSpec((width, low), lambda h: (0, h)),
            pl.BlockSpec((1, low), lambda h: (0, h)),
        ],
        out_shape=(
            jax.ShapeDtypeStruct((width, highs * low), f32),
            jax.ShapeDtypeStruct((1, highs * low), f32),
        ),
        scratch_shapes=[pltpu.VMEM((width, bags), bf16), pltpu.VMEM((width, bags), bf16)],
        compiler_params=params(),
        cost_estimate=pl.CostEstimate(flops=int(8e9), bytes_accessed=10 << 20, transcendentals=0),
        name="steps_of",
    )(grad, count, old)


def place_body(old_ref, step_ref, tgt_srt_ref, tgt_ref, out_ref, oh_ref, ol_ref, sh_ref, sl_ref):
    width, n = old_ref.shape
    tile = 256

    @pl.when(pl.program_id(0) == 0)
    def _():
        def cut(i, carry):
            at = pl.ds(pl.multiple_of(i * 32, 32), 32)
            oh_ref[at, :], ol_ref[at, :] = split(old_ref[at, :])
            sh_ref[at, :], sl_ref[at, :] = split(-step_ref[at, :])
            return carry

        lax.fori_loop(0, width // 32, cut, 0)

    slot = lax.broadcasted_iota(i32, (CAP, n), 0) + pl.program_id(0) * CAP
    old_at = jnp.where(slot == tgt_srt_ref[...], 1.0, 0.0).astype(bf16)
    step_at = jnp.where(slot == tgt_ref[...], 1.0, 0.0).astype(bf16)

    def one(i, carry):
        at = pl.ds(pl.multiple_of(i * tile, tile), tile)
        total = lax.dot_general(oh_ref[at, :], old_at, NT, preferred_element_type=f32)
        total = total + lax.dot_general(ol_ref[at, :], old_at, NT, preferred_element_type=f32)
        total = total + lax.dot_general(sh_ref[at, :], step_at, NT, preferred_element_type=f32)
        total = total + lax.dot_general(sl_ref[at, :], step_at, NT, preferred_element_type=f32)
        out_ref[0, at, :] = total
        return carry

    lax.fori_loop(0, width // tile, one, 0)


def place(old, step, tgt_srt, tgt, owners):
    width, n = old.shape
    whole = lambda shape: pl.BlockSpec(shape, lambda o: (0, 0))
    return pl.pallas_call(
        place_body,
        grid=(owners,),
        in_specs=[whole((width, n)), whole((width, n)), whole((1, n)), whole((1, n))],
        out_specs=pl.BlockSpec((1, width, CAP), lambda o: (o, 0, 0)),
        out_shape=jax.ShapeDtypeStruct((owners, width, CAP), f32),
        scratch_shapes=[pltpu.VMEM((width, n), bf16)] * 4,
        compiler_params=params(),
        cost_estimate=pl.CostEstimate(flops=int(8e9), bytes_accessed=8 << 20, transcendentals=0),
        name="place",
    )(old, step, tgt_srt, tgt)


def local(table, accum, grad_pooled, bag_of, slots, dirty_rows, owner):
    width_slice, bags = grad_pooled.shape
    col_count = lax.axis_size("col")
    row_count = lax.axis_size("row")
    col = lax.axis_index("col")
    n = dirty_rows.shape[1] // col_count
    rows = lax.dynamic_slice_in_dim(dirty_rows[0], col * n, n)
    owners = lax.dynamic_slice_in_dim(owner[:, 0], col * n, n)
    grad = lax.all_gather(grad_pooled, "col", axis=0, tiled=True)
    srt, tgt, tgt_srt, accum_old = plan(rows, owners, accum)
    srt_all = lax.all_gather(srt[0], "col", axis=0)
    count = pair_counts(bag_of[0], slots[0], col, bags, n)
    picked = gather_rows(table, srt_all)
    old = lax.all_to_all(picked, "col", 0, 0, tiled=True)
    old = old.reshape(width_slice * col_count, n)
    step, accum_new = steps_of(grad, count, accum_old)
    placed = place(old, step, tgt_srt, tgt, row_count)
    received = lax.all_to_all(placed, "row", 0, 0, tiled=True)
    owned = jnp.transpose(received, (1, 0, 2)).reshape(width_slice * col_count, row_count * CAP)
    return owned, accum_new[0]


def solution(mesh):
    return jax.shard_map(
        local,
        mesh=mesh,
        in_specs=(
            P("col", "row"),
            P("row"),
            P("col", "row"),
            P("row", None),
            P("row", None),
            P("row", None),
            P("row", None),
        ),
        out_specs=(P(None, ("row", "col")), P(("row", "col"))),
        check_vma=False,
    )
```

```python
import jax
import jax.numpy as jnp
from jax import lax
from jax.experimental import pallas as pl
from jax.experimental.pallas import tpu as pltpu
from jax.sharding import PartitionSpec as P

learn_rate = 0.3
epsilon = 1e-08

LANES = 128
CAP = 256
CHUNK = 512
BAGS = 64
PAIRS = 5
LOW = 256
VMEM_LIMIT = 48 * 1024 * 1024

f32, bf16, i32 = jnp.float32, jnp.bfloat16, jnp.int32
NT = (((1,), (1,)), ((), ()))
NN = (((1,), (0,)), ((), ()))


def split(x):
    high = x.astype(bf16)
    return high, (x - high.astype(f32)).astype(bf16)


def params(limit=VMEM_LIMIT):
    return pltpu.CompilerParams(vmem_limit_bytes=limit)


def plan_body(row_ref, own_ref, own_col_ref, accum_ref, tgt_ref, acc_ref):
    n = row_ref.shape[1]
    step = 256
    row, own = row_ref[...], own_ref[...]
    place = jnp.zeros((1, n), i32)
    lane = lax.broadcasted_iota(i32, (step, n), 1)
    for i in range(0, n, step):
        at = lax.broadcasted_iota(i32, (step, n), 0) + i
        same = (own == own_col_ref[i : i + step, :]) & (at < lane)
        place = place + jnp.sum(jnp.where(same, 1, 0), axis=0, keepdims=True)
    tgt_ref[...] = own * CAP + place
    tall = accum_ref.shape[1]
    picker = jnp.where(
        lax.broadcasted_iota(i32, (tall, n), 0) == row // LANES, 1.0, 0.0
    )
    wide = lax.dot_general(
        accum_ref[...], picker, NN, precision=lax.Precision.HIGHEST, preferred_element_type=f32
    )
    keep = lax.broadcasted_iota(i32, (LANES, n), 0) == row % LANES
    acc_ref[...] = jnp.sum(jnp.where(keep, wide, 0.0), axis=0, keepdims=True)


def plan(rows, owners, accum):
    n = rows.shape[0]
    return pl.pallas_call(
        plan_body,
        out_shape=(jax.ShapeDtypeStruct((1, n), i32), jax.ShapeDtypeStruct((1, n), f32)),
        compiler_params=params(),
        name="plan",
    )(rows[None, :], owners[None, :], owners[:, None], accum.reshape(-1, LANES).T)


def counts_body(chunk_ref, window_ref, block_ref, bag_ref, slot_ref, out_ref):
    highs, bags, low = out_ref.shape
    span = highs * low
    rows = highs * BAGS
    pairs = chunk_ref.shape[0]
    chunk = bag_ref.shape[1]

    def clear(i, carry):
        for h in range(highs):
            out_ref[h, pl.ds(pl.multiple_of(i * BAGS, BAGS), BAGS), :] = jnp.zeros(
                (BAGS, low), bf16
            )
        return carry

    lax.fori_loop(0, bags // BAGS, clear, 0)
    start = block_ref[0] * span
    left_iota = lax.broadcasted_iota(i32, (rows, chunk), 0).astype(f32).astype(bf16)
    right_iota = lax.broadcasted_iota(i32, (low, chunk), 0).astype(f32).astype(bf16)
    one, zero = jnp.ones((), bf16), jnp.zeros((), bf16)

    def some(j, carry):
        done = []
        for u in range(PAIRS):
            i, w = chunk_ref[j * PAIRS + u], window_ref[j * PAIRS + u]
            slot = slot_ref[pl.ds(i, 1), :] - start
            near = bag_ref[pl.ds(i, 1), :] - w * BAGS
            inside = (slot >= 0) & (slot < span) & (near >= 0) & (near < BAGS)
            left_id = jnp.where(inside, (slot // low) * BAGS + near, -1)
            left_id = left_id.astype(f32).astype(bf16)
            right_id = (slot & (low - 1)).astype(f32).astype(bf16)
            left = jnp.where(left_iota == left_id, one, zero)
            right = jnp.where(right_iota == right_id, one, zero)
            done.append((w, lax.dot_general(left, right, NT, preferred_element_type=f32)))
        for w, both in done:
            at = pl.ds(pl.multiple_of(w * BAGS, BAGS), BAGS)
            for h in range(highs):
                piece = both[h * BAGS : (h + 1) * BAGS].astype(bf16)
                out_ref[h, at, :] = out_ref[h, at, :] + piece
        return carry

    lax.fori_loop(0, pairs // PAIRS, some, 0)


def pair_counts(bag_of, slots, block, bags, span):
    chunks = bag_of.shape[0] // CHUNK
    bag = bag_of.reshape(chunks, CHUNK)
    total = chunks + bags // BAGS - 1
    assert total % PAIRS == 0
    ends = jnp.arange(chunks, dtype=i32) + bag[:, CHUNK - 1] // BAGS
    order = jnp.arange(total, dtype=i32)
    at_chunk = jnp.sum((ends[None, :] < order[:, None]).astype(i32), axis=1)
    at_window = order - at_chunk
    smem = pl.BlockSpec(memory_space=pltpu.SMEM)
    vmem = pl.BlockSpec(memory_space=pltpu.VMEM)
    return pl.pallas_call(
        counts_body,
        out_shape=jax.ShapeDtypeStruct((span // LOW, bags, LOW), bf16),
        in_specs=[smem, smem, smem, vmem, vmem],
        out_specs=vmem,
        compiler_params=params(),
        cost_estimate=pl.CostEstimate(flops=int(8e9), bytes_accessed=5 << 20, transcendentals=0),
        name="pair_counts",
    )(at_chunk, at_window, block[None], bag, slots.reshape(chunks, CHUNK))


def gather_body(row_ref, part_ref, table_ref, out_ref, tall_ref, stage_ref):
    width, columns = table_ref.shape
    parts = LANES // width
    height = columns // parts
    blocks, _, n = out_ref.shape
    per = n // LANES
    tiles = blocks * per

    def turn(i, carry):
        at = pl.multiple_of(i * LANES, LANES)
        wide = [table_ref[:, pl.ds(pl.multiple_of(q * height + at, LANES), LANES)] for q in range(parts)]
        tall_ref[pl.ds(at, LANES), :] = jnp.concatenate(wide, axis=0).T
        return carry

    lax.fori_loop(0, height // LANES, turn, 0, unroll=2)

    def fetch(t, slot):
        for u in range(LANES):
            row = row_ref[t * LANES + u] & (height - 1)
            stage_ref[slot, u : u + 1, :] = tall_ref[pl.ds(row, 1), :]

    def emit(t, slot):
        flat = stage_ref[slot].T
        part = part_ref[pl.ds(t, 1), :] // height
        picked = flat[:width]
        for q in range(1, parts):
            picked = jnp.where(part == q, flat[q * width : (q + 1) * width], picked)
        at = pl.ds(pl.multiple_of((t % per) * LANES, LANES), LANES)
        out_ref[t // per, :, at] = picked

    fetch(0, 0)

    def two(i, carry):
        fetch(2 * i + 1, 1)
        emit(2 * i, 0)
        fetch(jnp.minimum(2 * i + 2, tiles - 1), 0)
        emit(2 * i + 1, 1)
        return carry

    lax.fori_loop(0, tiles // 2, two, 0)


def gather_rows(table, rows, blocks):
    width, columns = table.shape
    n = rows.shape[0] // blocks
    vmem = pl.BlockSpec(memory_space=pltpu.VMEM)
    return pl.pallas_call(
        gather_body,
        in_specs=[pl.BlockSpec(memory_space=pltpu.SMEM), vmem, vmem],
        out_specs=vmem,
        out_shape=jax.ShapeDtypeStruct((blocks, width, n), f32),
        scratch_shapes=[
            pltpu.VMEM((columns * width // LANES, LANES), f32),
            pltpu.VMEM((2, LANES, LANES), f32),
        ],
        compiler_params=params(),
        cost_estimate=pl.CostEstimate(flops=int(1e9), bytes_accessed=10 << 20, transcendentals=0),
        name="gather_rows",
    )(rows, rows.reshape(-1, LANES), table)


def step_body(grad_ref, count_ref, old_ref, step_ref, new_ref, high_ref, low_ref):
    width = grad_ref.shape[0]
    tile = 256

    @pl.when(pl.program_id(0) == 0)
    def _():
        def cut(i, carry):
            at = pl.ds(pl.multiple_of(i * 32, 32), 32)
            high_ref[at, :], low_ref[at, :] = split(grad_ref[at, :])
            return carry

        lax.fori_loop(0, width // 32, cut, 0)

    count = count_ref[0]

    def one(i, total):
        at = pl.ds(pl.multiple_of(i * tile, tile), tile)
        grads = lax.dot_general(high_ref[at, :], count, NN, preferred_element_type=f32)
        grads = grads + lax.dot_general(low_ref[at, :], count, NN, preferred_element_type=f32)
        step_ref[at, :] = grads
        return total + jnp.sum(grads * grads, axis=0, keepdims=True)

    low = count.shape[1]
    total = lax.fori_loop(0, width // tile, one, jnp.zeros((1, low), f32))
    new = old_ref[...] + total / width
    new_ref[...] = new
    factor = learn_rate / (jnp.sqrt(new) + epsilon)
    step_ref[...] = step_ref[...] * factor


def steps_of(grad, count, old):
    width, bags = grad.shape
    highs, _, low = count.shape
    return pl.pallas_call(
        step_body,
        grid=(highs,),
        in_specs=[
            pl.BlockSpec((width, bags), lambda h: (0, 0)),
            pl.BlockSpec((1, bags, low), lambda h: (h, 0, 0)),
            pl.BlockSpec((1, low), lambda h: (0, h)),
        ],
        out_specs=[
            pl.BlockSpec((width, low), lambda h: (0, h)),
            pl.BlockSpec((1, low), lambda h: (0, h)),
        ],
        out_shape=(
            jax.ShapeDtypeStruct((width, highs * low), f32),
            jax.ShapeDtypeStruct((1, highs * low), f32),
        ),
        scratch_shapes=[pltpu.VMEM((width, bags), bf16), pltpu.VMEM((width, bags), bf16)],
        compiler_params=params(),
        cost_estimate=pl.CostEstimate(flops=int(8e9), bytes_accessed=10 << 20, transcendentals=0),
        name="steps_of",
    )(grad, count, old)


def place_body(old_ref, step_ref, tgt_ref, out_ref, high_ref, low_ref):
    width, n = old_ref.shape
    tile = 256

    @pl.when(pl.program_id(0) == 0)
    def _():
        def cut(i, carry):
            at = pl.ds(pl.multiple_of(i * 32, 32), 32)
            high_ref[at, :], low_ref[at, :] = split(old_ref[at, :] - step_ref[at, :])
            return carry

        lax.fori_loop(0, width // 32, cut, 0)

    slot = lax.broadcasted_iota(i32, (CAP, n), 0) + pl.program_id(0) * CAP
    here = jnp.where(slot == tgt_ref[...], 1.0, 0.0).astype(bf16)

    def one(i, carry):
        at = pl.ds(pl.multiple_of(i * tile, tile), tile)
        total = lax.dot_general(high_ref[at, :], here, NT, preferred_element_type=f32)
        total = total + lax.dot_general(low_ref[at, :], here, NT, preferred_element_type=f32)
        out_ref[0, at, :] = total
        return carry

    lax.fori_loop(0, width // tile, one, 0)


def place(old, step, tgt, owners):
    width, n = old.shape
    whole = lambda shape: pl.BlockSpec(shape, lambda o: (0, 0))
    return pl.pallas_call(
        place_body,
        grid=(owners,),
        in_specs=[whole((width, n)), whole((width, n)), whole((1, n))],
        out_specs=pl.BlockSpec((1, width, CAP), lambda o: (o, 0, 0)),
        out_shape=jax.ShapeDtypeStruct((owners, width, CAP), f32),
        scratch_shapes=[pltpu.VMEM((width, n), bf16)] * 2,
        compiler_params=params(),
        cost_estimate=pl.CostEstimate(flops=int(4e9), bytes_accessed=8 << 20, transcendentals=0),
        name="place",
    )(old, step, tgt)


def join_body(part_ref, out_ref):
    out_ref[...] = part_ref[0]


def join(parts):
    count, width, cap = parts.shape
    return pl.pallas_call(
        join_body,
        grid=(count,),
        in_specs=[pl.BlockSpec((1, width, cap), lambda s: (s, 0, 0))],
        out_specs=pl.BlockSpec((width, cap), lambda s: (0, s)),
        out_shape=jax.ShapeDtypeStruct((width, count * cap), f32),
        name="join",
    )(parts)


def local(table, accum, grad_pooled, bag_of, slots, dirty_rows, owner):
    width_slice, bags = grad_pooled.shape
    col_count = lax.axis_size("col")
    row_count = lax.axis_size("row")
    col = lax.axis_index("col")
    n = dirty_rows.shape[1] // col_count
    rows = lax.dynamic_slice_in_dim(dirty_rows[0], col * n, n)
    owners = lax.dynamic_slice_in_dim(owner[:, 0], col * n, n)
    grad = lax.all_gather(grad_pooled, "col", axis=0, tiled=True)
    tgt, accum_old = plan(rows, owners, accum)
    picked = gather_rows(table, dirty_rows[0], col_count)
    old = lax.all_to_all(picked, "col", 0, 0, tiled=True)
    old = old.reshape(width_slice * col_count, n)
    count = pair_counts(bag_of[0], slots[0], col, bags, n)
    step, accum_new = steps_of(grad, count, accum_old)
    placed = place(old, step, tgt, row_count)
    owned = join(lax.all_to_all(placed, "row", 0, 0, tiled=True))
    return owned, accum_new[0]


def solution(mesh):
    return jax.shard_map(
        local,
        mesh=mesh,
        in_specs=(
            P("col", "row"),
            P("row"),
            P("col", "row"),
            P("row", None),
            P("row", None),
            P("row", None),
            P("row", None),
        ),
        out_specs=(P(None, ("row", "col")), P(("row", "col"))),
        check_vma=False,
    )
```

```python
import functools

import jax
import jax.numpy as jnp
from jax import lax
from jax.experimental import pallas as pl
from jax.experimental.pallas import tpu as pltpu
from jax.sharding import PartitionSpec as P

learn_rate = 0.3
epsilon = 1e-08

LANES = 128
CAP = 256
CHUNK = 512
BAGS = 64
PAIRS = 5
LOW = 256
SHARES = 2

f32, bf16, i32 = jnp.float32, jnp.bfloat16, jnp.int32
NT = (((1,), (1,)), ((), ()))
NN = (((1,), (0,)), ((), ()))


def split(x):
    high = x.astype(bf16)
    return high, (x - high.astype(f32)).astype(bf16)


def params(mib):
    return pltpu.CompilerParams(vmem_limit_bytes=mib * 1024 * 1024)


SMEM = pl.BlockSpec(memory_space=pltpu.SMEM)
VMEM = pl.BlockSpec(memory_space=pltpu.VMEM)
ANY = pl.BlockSpec(memory_space=pl.ANY)
HBM = pl.BlockSpec(memory_space=pltpu.HBM)


def plan_body(col_ref, row_ref, own_ref, accum_ref, tgt_ref, acc_ref):
    n = row_ref.shape[1]
    row, own = row_ref[...], own_ref[...]
    named = jnp.where(lax.broadcasted_iota(i32, (8, n), 0) == own, 1.0, 0.0)
    earlier = lax.broadcasted_iota(i32, (n, n), 0) < lax.broadcasted_iota(i32, (n, n), 1)
    earlier = jnp.where(earlier, 1.0, 0.0).astype(bf16)
    before = lax.dot_general(named.astype(bf16), earlier, NN, preferred_element_type=f32)
    place = jnp.sum(named * before, axis=0, keepdims=True).astype(i32)
    tgt_ref[...] = own * CAP + place
    tall = accum_ref.shape[0]
    picker = jnp.where(
        lax.broadcasted_iota(i32, (tall, n), 0) == row // LANES, 1.0, 0.0
    )
    wide = lax.dot_general(
        accum_ref[...].T, picker, NN, precision=lax.Precision.HIGHEST, preferred_element_type=f32
    )
    keep = lax.broadcasted_iota(i32, (LANES, n), 0) == row % LANES
    acc_ref[...] = jnp.sum(jnp.where(keep, wide, 0.0), axis=0, keepdims=True)


def plan(col, rows, owners, accum, blocks):
    assert blocks % 8 == 0
    n = rows.shape[1] // blocks
    accum = accum.reshape(-1, LANES)
    own = lambda i, c: (0, c[0])
    return pl.pallas_call(
        plan_body,
        grid_spec=pltpu.PrefetchScalarGridSpec(
            num_scalar_prefetch=1,
            grid=(1,),
            in_specs=[
                pl.BlockSpec((1, n), own),
                pl.BlockSpec((1, n), own),
                pl.BlockSpec(accum.shape, lambda i, c: (0, 0)),
            ],
            out_specs=[pl.BlockSpec((1, n), lambda i, c: (0, 0))] * 2,
        ),
        out_shape=(jax.ShapeDtypeStruct((1, n), i32), jax.ShapeDtypeStruct((1, n), f32)),
        compiler_params=params(16),
        name="plan",
    )(col[None], rows, owners, accum)


def counts_body(block_ref, end_ref, bag_ref, slot_ref, out_ref):
    highs, bags, low = out_ref.shape
    span = highs * low
    rows = highs * BAGS
    chunks = bag_ref.shape[1] // CHUNK
    pairs = chunks + bags // BAGS - 1
    assert pairs % PAIRS == 0

    def clear(i, carry):
        for h in range(highs):
            out_ref[h, pl.ds(pl.multiple_of(i * BAGS, BAGS), BAGS), :] = jnp.zeros(
                (BAGS, low), bf16
            )
        return carry

    lax.fori_loop(0, bags // BAGS, clear, 0)
    start = block_ref[0] * span
    left_iota = lax.broadcasted_iota(i32, (rows, CHUNK), 0).astype(f32).astype(bf16)
    right_iota = lax.broadcasted_iota(i32, (low, CHUNK), 0).astype(f32).astype(bf16)
    one, zero = jnp.ones((), bf16), jnp.zeros((), bf16)

    def some(j, carry):
        i, w = carry
        done = []
        for u in range(PAIRS):
            at = pl.ds(pl.multiple_of(i * CHUNK, CHUNK), CHUNK)
            slot = slot_ref[:, at] - start
            near = bag_ref[:, at] - w * BAGS
            inside = (slot >= 0) & (slot < span) & (near >= 0) & (near < BAGS)
            left_id = jnp.where(inside, (slot // low) * BAGS + near, -1)
            left_id = left_id.astype(f32).astype(bf16)
            right_id = (slot & (low - 1)).astype(f32).astype(bf16)
            left = jnp.where(left_iota == left_id, one, zero)
            right = jnp.where(right_iota == right_id, one, zero)
            done.append((w, lax.dot_general(left, right, NT, preferred_element_type=f32)))
            more = w < end_ref[0, i * CHUNK + CHUNK - 1] // BAGS
            i, w = (
                jnp.where(more, i, jnp.minimum(i + 1, chunks - 1)),
                jnp.where(more, w + 1, w),
            )
        for v, both in done:
            at = pl.ds(pl.multiple_of(v * BAGS, BAGS), BAGS)
            for h in range(highs):
                piece = both[h * BAGS : (h + 1) * BAGS].astype(bf16)
                out_ref[h, at, :] = out_ref[h, at, :] + piece
        return i, w

    lax.fori_loop(0, pairs // PAIRS, some, (0, 0))


def pair_counts(bag_of, slots, block, bags, span):
    smem = pl.BlockSpec(memory_space=pltpu.SMEM)
    vmem = pl.BlockSpec(memory_space=pltpu.VMEM)
    return pl.pallas_call(
        counts_body,
        out_shape=jax.ShapeDtypeStruct((span // LOW, bags, LOW), bf16),
        in_specs=[smem, smem, vmem, vmem],
        out_specs=vmem,
        compiler_params=params(12),
        cost_estimate=pl.CostEstimate(flops=int(8e9), bytes_accessed=5 << 20, transcendentals=0),
        name="pair_counts",
    )(block[None], bag_of, bag_of, slots)


def gather_body(row_ref, part_ref, table_ref, after_ref, *refs):
    out_refs, (tall_ref, stage_ref) = refs[:SHARES], refs[SHARES:]
    width, columns = table_ref.shape
    parts = LANES // width
    height = columns // parts
    blocks, narrow, n = out_refs[0].shape
    per = n // LANES
    tiles = blocks * per

    def turn(i, carry):
        at = pl.multiple_of(i * LANES, LANES)
        wide = [table_ref[:, pl.ds(pl.multiple_of(q * height + at, LANES), LANES)] for q in range(parts)]
        tall_ref[pl.ds(at, LANES), :] = jnp.concatenate(wide, axis=0).T
        return carry

    lax.fori_loop(0, height // LANES, turn, 0, unroll=2)

    def fetch(t, slot):
        for u in range(LANES):
            row = row_ref[0, t * LANES + u] & (height - 1)
            stage_ref[slot, u : u + 1, :] = tall_ref[pl.ds(row, 1), :]

    def emit(t, slot):
        flat = stage_ref[slot].T
        part = part_ref[:, pl.ds(pl.multiple_of(t * LANES, LANES), LANES)] // height
        picked = flat[:width]
        for q in range(1, parts):
            picked = jnp.where(part == q, flat[q * width : (q + 1) * width], picked)
        at = pl.ds(pl.multiple_of((t % per) * LANES, LANES), LANES)
        for h, out_ref in enumerate(out_refs):
            out_ref[t // per, :, at] = picked[h * narrow : (h + 1) * narrow]

    fetch(0, 0)

    def two(i, carry):
        fetch(2 * i + 1, 1)
        emit(2 * i, 0)
        fetch(jnp.minimum(2 * i + 2, tiles - 1), 0)
        emit(2 * i + 1, 1)
        return carry

    lax.fori_loop(0, tiles // 2, two, 0)


def gather_rows(table, rows, blocks, after):
    width, columns = table.shape
    n = rows.shape[1] // blocks
    return pl.pallas_call(
        gather_body,
        in_specs=[SMEM, VMEM, VMEM, ANY],
        out_specs=[VMEM] * SHARES,
        out_shape=(jax.ShapeDtypeStruct((blocks, width // SHARES, n), f32),) * SHARES,
        scratch_shapes=[
            pltpu.VMEM((columns * width // LANES, LANES), f32),
            pltpu.VMEM((2, LANES, LANES), f32),
        ],
        compiler_params=params(24),
        cost_estimate=pl.CostEstimate(flops=int(1e9), bytes_accessed=10 << 20, transcendentals=0),
        name="gather_rows",
    )(rows, rows, table, after)


def step_body(grad_ref, count_ref, old_ref, step_ref, new_ref, high_ref, low_ref):
    width = grad_ref.shape[0]
    tile = 256

    @pl.when(pl.program_id(0) == 0)
    def _():
        def cut(i, carry):
            at = pl.ds(pl.multiple_of(i * 32, 32), 32)
            high_ref[at, :], low_ref[at, :] = split(grad_ref[at, :])
            return carry

        lax.fori_loop(0, width // 32, cut, 0)

    count = count_ref[0]

    def one(i, total):
        at = pl.ds(pl.multiple_of(i * tile, tile), tile)
        grads = lax.dot_general(high_ref[at, :], count, NN, preferred_element_type=f32)
        grads = grads + lax.dot_general(low_ref[at, :], count, NN, preferred_element_type=f32)
        step_ref[at, :] = grads
        return total + jnp.sum(grads * grads, axis=0, keepdims=True)

    low = count.shape[1]
    total = lax.fori_loop(0, width // tile, one, jnp.zeros((1, low), f32))
    new = old_ref[...] + total / width
    new_ref[...] = new
    factor = learn_rate / (jnp.sqrt(new) + epsilon)
    step_ref[...] = step_ref[...] * factor


def steps_of(grad, count, old):
    width, bags = grad.shape
    highs, _, low = count.shape
    return pl.pallas_call(
        step_body,
        grid=(highs,),
        in_specs=[
            pl.BlockSpec((width, bags), lambda h: (0, 0)),
            pl.BlockSpec((1, bags, low), lambda h: (h, 0, 0)),
            pl.BlockSpec((1, low), lambda h: (0, h)),
        ],
        out_specs=[
            pl.BlockSpec((width, low), lambda h: (0, h)),
            pl.BlockSpec((1, low), lambda h: (0, h)),
        ],
        out_shape=(
            jax.ShapeDtypeStruct((width, highs * low), f32),
            jax.ShapeDtypeStruct((1, highs * low), f32),
        ),
        scratch_shapes=[pltpu.VMEM((width, bags), bf16), pltpu.VMEM((width, bags), bf16)],
        compiler_params=params(20),
        cost_estimate=pl.CostEstimate(flops=int(8e9), bytes_accessed=10 << 20, transcendentals=0),
        name="steps_of",
    )(grad, count, old)


def place_body(share, dest_ref, old_ref, step_ref, tgt_ref, after_ref, *refs):
    out_refs, (high_ref, low_ref, hold_ref, sems) = refs[:-4], refs[-4:]
    slices, narrow, n = old_ref.shape
    tgt = tgt_ref[...]

    def cut(f, carry):
        step = step_ref[pl.ds(pl.multiple_of((f * SHARES + share) * narrow, narrow), narrow), :]
        at = pl.ds(pl.multiple_of(f * narrow, narrow), narrow)
        high_ref[at, :], low_ref[at, :] = split(old_ref[f] - step)
        return carry

    lax.fori_loop(0, slices, cut, 0)
    slot = lax.broadcasted_iota(i32, (CAP, n), 0)
    copies = []
    for i, out_ref in enumerate(out_refs):
        here = jnp.where(slot == tgt - dest_ref[i] * CAP, 1.0, 0.0).astype(bf16)
        total = lax.dot_general(high_ref[...], here, NT, preferred_element_type=f32)
        total = total + lax.dot_general(low_ref[...], here, NT, preferred_element_type=f32)
        hold_ref[i] = total
        copies.append(pltpu.make_async_copy(hold_ref.at[i], out_ref, sems.at[i]))
        copies[-1].start()
    for copy in copies:
        copy.wait()


def place(share, dests, old, step, tgt, after):
    count = dests.shape[0]
    rows = old.shape[0] * old.shape[1]
    half = pltpu.VMEM((rows, old.shape[2]), bf16)
    return pl.pallas_call(
        functools.partial(place_body, share),
        in_specs=[SMEM, VMEM, VMEM, VMEM, ANY],
        out_specs=[HBM] * count,
        out_shape=(jax.ShapeDtypeStruct((rows, CAP), f32),) * count,
        scratch_shapes=[
            half,
            half,
            pltpu.VMEM((count, rows, CAP), f32),
            pltpu.SemaphoreType.DMA((count,)),
        ],
        compiler_params=params(12),
        cost_estimate=pl.CostEstimate(flops=int(2e9), bytes_accessed=6 << 20, transcendentals=0),
        name="place",
    )(dests, old, step, tgt, after)


def join_body(shares, at_ref, *refs):
    count = len(shares)
    parts, (out_ref, hold_ref, in_sems, out_sems) = refs[:count], refs[-4:]
    cap = hold_ref.shape[3]
    loads, stores = [], []
    for i, share in enumerate(shares):
        loads.append(pltpu.make_async_copy(parts[i], hold_ref.at[i], in_sems.at[i]))
        to = out_ref.at[:, share, :, pl.ds(pl.multiple_of(at_ref[i] * cap, cap), cap)]
        stores.append(pltpu.make_async_copy(hold_ref.at[i], to, out_sems.at[i]))
    for load in loads:
        load.start()
    for load, store in zip(loads, stores):
        load.wait()
        store.start()
    for store in stores:
        store.wait()


def join(shares, at, parts, whole, total, slices):
    count = len(parts)
    rows, cap = parts[0].shape
    narrow = rows // slices
    parts = [part.reshape(slices, narrow, cap) for part in parts]
    kept = () if whole is None else (whole,)
    return pl.pallas_call(
        functools.partial(join_body, shares),
        in_specs=[SMEM] + [HBM] * (count + len(kept)),
        out_specs=HBM,
        out_shape=jax.ShapeDtypeStruct((slices, SHARES, narrow, total * cap), f32),
        scratch_shapes=[
            pltpu.VMEM((count, slices, narrow, cap), f32),
            pltpu.SemaphoreType.DMA((count,)),
            pltpu.SemaphoreType.DMA((count,)),
        ],
        input_output_aliases={1 + count: 0} if kept else {},
        compiler_params=params(4),
        cost_estimate=pl.CostEstimate(flops=0, bytes_accessed=count << 19, transcendentals=0),
        name="join",
    )(jnp.stack(at), *parts, *kept)


def exchange(olds, step, tgt):
    count = lax.axis_size("row")
    chips, cores = count // 2, 2
    me = lax.axis_index("row")
    slices = olds[0].shape[0]

    def toward(dy, dc, of):
        y, core = of // cores, of % cores
        return (y + dy) % chips * cores + (core + dc) % cores

    def send(part, dy, dc):
        if (dy, dc) == (0, 0):
            return part
        return lax.ppermute(part, "row", [(s, toward(dy, dc, s)) for s in range(count)])

    near = [(1, 0), (chips - 1, 0), (1, 1), (chips - 1, 1)]
    far = [(dy, dc) for dy in range(2, chips - 1) for dc in range(2)]
    own = [(0, 1), (0, 0)]
    shifts = near + far + own
    dests = jnp.stack([toward(dy, dc, me) for dy, dc in shifts])
    got, made = {}, [tgt]
    for h, old in enumerate(olds):
        made = place(h, dests, old, step, tgt, made[0])
        for part, shift in zip(made, shifts):
            got[h, shift] = send(part, *shift)
    groups = []
    for h in range(SHARES):
        last = h == SHARES - 1
        groups.append([(h, shift) for shift in near + (own if last else [])])
        groups.append([(h, shift) for shift in far + ([] if last else own)])
    whole = None
    for group in groups:
        at = [toward(chips - dy, cores - dc, me) for _, (dy, dc) in group]
        whole = join(tuple(h for h, _ in group), at, [got[key] for key in group], whole, count, slices)
    return whole.reshape(-1, count * CAP)


def local(table, accum, grad_pooled, bag_of, slots, dirty_rows, owner):
    width_slice, bags = grad_pooled.shape
    col_count = lax.axis_size("col")
    col = lax.axis_index("col")
    n = dirty_rows.shape[1] // col_count
    grad = lax.all_gather(grad_pooled, "col", axis=0, tiled=True)
    tgt, accum_old = plan(col, dirty_rows, owner.T, accum, col_count)
    count = pair_counts(bag_of, slots, col, bags, n)
    picked = gather_rows(table, dirty_rows, col_count, count)
    step, accum_new = steps_of(grad, count, accum_old)
    later, step = lax.optimization_barrier((tuple(picked[1:]), step))
    olds = [lax.all_to_all(part, "col", 0, 0, tiled=True) for part in (picked[0], *later)]
    owned = exchange(olds, step, tgt)
    return owned, accum_new[0]


def solution(mesh):
    return jax.shard_map(
        local,
        mesh=mesh,
        in_specs=(
            P("col", "row"),
            P("row"),
            P("col", "row"),
            P("row", None),
            P("row", None),
            P("row", None),
            P("row", None),
        ),
        out_specs=(P(None, ("row", "col")), P(("row", "col"))),
        check_vma=False,
    )
```

```python
import functools

import jax
import jax.numpy as jnp
from jax import lax
from jax.experimental import pallas as pl
from jax.experimental.pallas import tpu as pltpu
from jax.sharding import PartitionSpec as P

learn_rate = 0.3
epsilon = 1e-08

LANES = 128
CAP = 256
CHUNK = 512
BAGS = 64
PAIRS = 5
LOW = 256
WHOLE = 60
JOIN = 4
SHARES = 2

f32, bf16, i32 = jnp.float32, jnp.bfloat16, jnp.int32
NT = (((1,), (1,)), ((), ()))
NN = (((1,), (0,)), ((), ()))


def split(x):
    high = x.astype(bf16)
    return high, (x - high.astype(f32)).astype(bf16)


def params(mib):
    return pltpu.CompilerParams(vmem_limit_bytes=mib * 1024 * 1024)


SMEM = pl.BlockSpec(memory_space=pltpu.SMEM)
VMEM = pl.BlockSpec(memory_space=pltpu.VMEM)
ANY = pl.BlockSpec(memory_space=pl.ANY)
HBM = pl.BlockSpec(memory_space=pltpu.HBM)


def plan_body(col_ref, row_ref, own_ref, accum_ref, tgt_ref, acc_ref):
    n = row_ref.shape[1]
    row, own = row_ref[...], own_ref[...]
    named = jnp.where(lax.broadcasted_iota(i32, (8, n), 0) == own, 1.0, 0.0)
    earlier = lax.broadcasted_iota(i32, (n, n), 0) < lax.broadcasted_iota(i32, (n, n), 1)
    earlier = jnp.where(earlier, 1.0, 0.0).astype(bf16)
    before = lax.dot_general(named.astype(bf16), earlier, NN, preferred_element_type=f32)
    place = jnp.sum(named * before, axis=0, keepdims=True).astype(i32)
    tgt_ref[...] = own * CAP + place
    tall = accum_ref.shape[0]
    picker = jnp.where(
        lax.broadcasted_iota(i32, (tall, n), 0) == row // LANES, 1.0, 0.0
    )
    wide = lax.dot_general(
        accum_ref[...].T, picker, NN, precision=lax.Precision.HIGHEST, preferred_element_type=f32
    )
    keep = lax.broadcasted_iota(i32, (LANES, n), 0) == row % LANES
    acc_ref[...] = jnp.sum(jnp.where(keep, wide, 0.0), axis=0, keepdims=True)


def plan(col, rows, owners, accum, blocks):
    assert blocks % 8 == 0
    n = rows.shape[1] // blocks
    accum = accum.reshape(-1, LANES)
    own = lambda i, c: (0, c[0])
    return pl.pallas_call(
        plan_body,
        grid_spec=pltpu.PrefetchScalarGridSpec(
            num_scalar_prefetch=1,
            grid=(1,),
            in_specs=[
                pl.BlockSpec((1, n), own),
                pl.BlockSpec((1, n), own),
                pl.BlockSpec(accum.shape, lambda i, c: (0, 0)),
            ],
            out_specs=[pl.BlockSpec((1, n), lambda i, c: (0, 0))] * 2,
        ),
        out_shape=(jax.ShapeDtypeStruct((1, n), i32), jax.ShapeDtypeStruct((1, n), f32)),
        compiler_params=params(16),
        name="plan",
    )(col[None], rows, owners, accum)


def counts_body(block_ref, end_ref, bag_ref, slot_ref, out_ref):
    highs, bags, low = out_ref.shape
    span = highs * low
    rows = highs * BAGS
    chunks = bag_ref.shape[1] // CHUNK
    pairs = chunks + bags // BAGS - 1
    assert pairs % PAIRS == 0

    def clear(i, carry):
        for h in range(highs):
            out_ref[h, pl.ds(pl.multiple_of(i * BAGS, BAGS), BAGS), :] = jnp.zeros(
                (BAGS, low), bf16
            )
        return carry

    lax.fori_loop(0, bags // BAGS, clear, 0)
    start = block_ref[0] * span
    left_iota = lax.broadcasted_iota(i32, (rows, CHUNK), 0).astype(f32).astype(bf16)
    right_iota = lax.broadcasted_iota(i32, (low, CHUNK), 0).astype(f32).astype(bf16)
    one, zero = jnp.ones((), bf16), jnp.zeros((), bf16)

    def some(j, carry):
        i, w = carry
        done = []
        for u in range(PAIRS):
            at = pl.ds(pl.multiple_of(i * CHUNK, CHUNK), CHUNK)
            slot = slot_ref[:, at] - start
            near = bag_ref[:, at] - w * BAGS
            inside = (slot >= 0) & (slot < span) & (near >= 0) & (near < BAGS)
            left_id = jnp.where(inside, (slot // low) * BAGS + near, -1)
            left_id = left_id.astype(f32).astype(bf16)
            right_id = (slot & (low - 1)).astype(f32).astype(bf16)
            left = jnp.where(left_iota == left_id, one, zero)
            right = jnp.where(right_iota == right_id, one, zero)
            done.append((w, lax.dot_general(left, right, NT, preferred_element_type=f32)))
            more = w < end_ref[0, i * CHUNK + CHUNK - 1] // BAGS
            i, w = (
                jnp.where(more, i, jnp.minimum(i + 1, chunks - 1)),
                jnp.where(more, w + 1, w),
            )
        for v, both in done:
            at = pl.ds(pl.multiple_of(v * BAGS, BAGS), BAGS)
            for h in range(highs):
                piece = both[h * BAGS : (h + 1) * BAGS].astype(bf16)
                out_ref[h, at, :] = out_ref[h, at, :] + piece
        return i, w

    lax.fori_loop(0, pairs // PAIRS, some, (0, 0))


def pair_counts(bag_of, slots, block, bags, span):
    smem = pl.BlockSpec(memory_space=pltpu.SMEM)
    vmem = pl.BlockSpec(memory_space=pltpu.VMEM)
    return pl.pallas_call(
        counts_body,
        out_shape=jax.ShapeDtypeStruct((span // LOW, bags, LOW), bf16),
        in_specs=[smem, smem, vmem, vmem],
        out_specs=vmem,
        compiler_params=params(12),
        cost_estimate=pl.CostEstimate(flops=int(8e9), bytes_accessed=5 << 20, transcendentals=0),
        name="pair_counts",
    )(block[None], bag_of, bag_of, slots)


def gather_body(row_ref, part_ref, table_ref, after_ref, *refs):
    out_refs, (tall_ref, stage_ref) = refs[:SHARES], refs[SHARES:]
    width, columns = table_ref.shape
    parts = LANES // width
    height = columns // parts
    blocks, narrow, n = out_refs[0].shape
    per = n // LANES
    tiles = blocks * per

    def turn(i, carry):
        at = pl.multiple_of(i * LANES, LANES)
        wide = [table_ref[:, pl.ds(pl.multiple_of(q * height + at, LANES), LANES)] for q in range(parts)]
        tall_ref[pl.ds(at, LANES), :] = jnp.concatenate(wide, axis=0).T
        return carry

    lax.fori_loop(0, height // LANES, turn, 0, unroll=2)

    def fetch(t, slot):
        for u in range(LANES):
            row = row_ref[0, t * LANES + u] & (height - 1)
            stage_ref[slot, u : u + 1, :] = tall_ref[pl.ds(row, 1), :]

    def emit(t, slot):
        flat = stage_ref[slot].T
        part = part_ref[:, pl.ds(pl.multiple_of(t * LANES, LANES), LANES)] // height
        picked = flat[:width]
        for q in range(1, parts):
            picked = jnp.where(part == q, flat[q * width : (q + 1) * width], picked)
        at = pl.ds(pl.multiple_of((t % per) * LANES, LANES), LANES)
        for h, out_ref in enumerate(out_refs):
            out_ref[t // per, :, at] = picked[h * narrow : (h + 1) * narrow]

    fetch(0, 0)

    def two(i, carry):
        fetch(2 * i + 1, 1)
        emit(2 * i, 0)
        fetch(jnp.minimum(2 * i + 2, tiles - 1), 0)
        emit(2 * i + 1, 1)
        return carry

    lax.fori_loop(0, tiles // 2, two, 0)


def gather_rows(table, rows, blocks, after):
    width, columns = table.shape
    n = rows.shape[1] // blocks
    return pl.pallas_call(
        gather_body,
        in_specs=[SMEM, VMEM, VMEM, ANY],
        out_specs=[VMEM] * SHARES,
        out_shape=(jax.ShapeDtypeStruct((blocks, width // SHARES, n), f32),) * SHARES,
        scratch_shapes=[
            pltpu.VMEM((columns * width // LANES, LANES), f32),
            pltpu.VMEM((2, LANES, LANES), f32),
        ],
        compiler_params=params(24),
        cost_estimate=pl.CostEstimate(flops=int(1e9), bytes_accessed=10 << 20, transcendentals=0),
        name="gather_rows",
    )(rows, rows, table, after)


def step_body(grad_ref, count_ref, old_ref, step_ref, new_ref, *scratch):
    wide_ref, both_ref, hold_ref, out_ref, grad_sems, count_sems, out_sems = scratch
    width, bags = grad_ref.shape
    highs, _, low = count_ref.shape
    cuts = grad_sems.shape[0]
    deep = width // cuts
    assert both_ref.shape == (cuts, 2 * deep, bags)
    grads = [
        pltpu.make_async_copy(
            grad_ref.at[i * deep : (i + 1) * deep, :],
            wide_ref.at[i * deep : (i + 1) * deep, :],
            grad_sems.at[i],
        )
        for i in range(cuts)
    ]
    counts = [
        pltpu.make_async_copy(count_ref.at[h], hold_ref.at[h], count_sems.at[h])
        for h in range(highs)
    ]
    outs = [
        pltpu.make_async_copy(
            out_ref.at[h], step_ref.at[:, h * low : (h + 1) * low], out_sems.at[h]
        )
        for h in range(highs)
    ]
    for copy in (*grads, counts[0]):
        copy.start()
    for i in range(cuts):
        grads[i].wait()
        if i == cuts - 1:
            for copy in counts[1:]:
                copy.start()

        def cut(j, carry):
            high, low = split(wide_ref[pl.ds(pl.multiple_of(i * deep + j * 32, 32), 32), :])
            both_ref[i, pl.ds(pl.multiple_of(j * 32, 32), 32), :] = high
            both_ref[i, pl.ds(pl.multiple_of(deep + j * 32, 32), 32), :] = low
            return carry

        lax.fori_loop(0, deep // 32, cut, 0)

    for h in range(highs):
        counts[h].wait()

        def one(i, total):
            got = lax.dot_general(both_ref[i], hold_ref[h], NN, preferred_element_type=f32)
            got = got[:deep] + got[deep:]
            out_ref[h, pl.ds(pl.multiple_of(i * deep, deep), deep), :] = got
            return total + jnp.sum(got * got, axis=0, keepdims=True)

        total = lax.fori_loop(0, cuts, one, jnp.zeros((1, low), f32))
        here = slice(h * low, (h + 1) * low)
        new = old_ref[:, here] + total / width
        new_ref[:, here] = new
        out_ref[h] = out_ref[h] * (learn_rate / (jnp.sqrt(new) + epsilon))
        outs[h].start()
    for copy in outs:
        copy.wait()


def steps_of(grad, count, old):
    width, bags = grad.shape
    highs, _, low = count.shape
    cuts = 2
    return pl.pallas_call(
        step_body,
        in_specs=[HBM, HBM, VMEM],
        out_specs=[HBM, VMEM],
        out_shape=(
            jax.ShapeDtypeStruct((width, highs * low), f32),
            jax.ShapeDtypeStruct((1, highs * low), f32),
        ),
        scratch_shapes=[
            pltpu.VMEM((width, bags), f32),
            pltpu.VMEM((cuts, 2 * width // cuts, bags), bf16),
            pltpu.VMEM(count.shape, bf16),
            pltpu.VMEM((highs, width, low), f32),
            pltpu.SemaphoreType.DMA((cuts,)),
            pltpu.SemaphoreType.DMA((highs,)),
            pltpu.SemaphoreType.DMA((highs,)),
        ],
        compiler_params=params(WHOLE),
        cost_estimate=pl.CostEstimate(flops=int(8e9), bytes_accessed=10 << 20, transcendentals=0),
        name="steps_of",
    )(grad, count, old)


def place_body(share, towards, me_ref, old_ref, step_ref, tgt_ref, after_ref, *refs):
    out_refs, scratch = refs[:-6], refs[-6:]
    old_hold, step_hold, both_ref, hold_ref, loads, sems = scratch
    slices, narrow, n = old_ref.shape
    rows = slices * narrow
    tgt = tgt_ref[...]
    old_copy = pltpu.make_async_copy(old_ref, old_hold, loads.at[0])
    step_copy = pltpu.make_async_copy(step_ref.at[:, share], step_hold, loads.at[1])
    old_copy.start()
    step_copy.start()
    old_copy.wait()
    step_copy.wait()

    def cut(f, carry):
        high, low = split(old_hold[f] - step_hold[f])
        both_ref[pl.ds(pl.multiple_of(f * narrow, narrow), narrow), :] = high
        both_ref[pl.ds(pl.multiple_of(rows + f * narrow, narrow), narrow), :] = low
        return carry

    lax.fori_loop(0, slices, cut, 0)
    slot = lax.broadcasted_iota(i32, (CAP, n), 0)
    copies = []
    for i, out_ref in enumerate(out_refs):
        here = jnp.where(slot == tgt - towards[i](me_ref[0]) * CAP, 1.0, 0.0).astype(bf16)
        total = lax.dot_general(both_ref[...], here, NT, preferred_element_type=f32)
        hold_ref[i] = total[:rows] + total[rows:]
        copies.append(pltpu.make_async_copy(hold_ref.at[i], out_ref, sems.at[i]))
        copies[-1].start()
    for copy in copies:
        copy.wait()


def place(share, towards, me, old, step, tgt, after):
    count = len(towards)
    rows = old.shape[0] * old.shape[1]
    return pl.pallas_call(
        functools.partial(place_body, share, towards),
        in_specs=[SMEM, HBM, HBM, VMEM, ANY],
        out_specs=[HBM] * count,
        out_shape=(jax.ShapeDtypeStruct((rows, CAP), f32),) * count,
        scratch_shapes=[
            pltpu.VMEM(old.shape, f32),
            pltpu.VMEM(old.shape, f32),
            pltpu.VMEM((2 * rows, old.shape[2]), bf16),
            pltpu.VMEM((count, rows, CAP), f32),
            pltpu.SemaphoreType.DMA((2,)),
            pltpu.SemaphoreType.DMA((count,)),
        ],
        compiler_params=params(WHOLE),
        cost_estimate=pl.CostEstimate(flops=int(2e9), bytes_accessed=6 << 20, transcendentals=0),
        name="place",
    )(me, old, step.reshape(old.shape[0], SHARES, *old.shape[1:]), tgt, after)


def join_body(shares, me_ref, *refs):
    count = len(shares)
    parts, (out_ref, hold_ref, in_sems, out_sems) = refs[:count], refs[-4:]
    cap = hold_ref.shape[3]
    loads, stores = [], []
    for i, (share, source) in enumerate(shares):
        loads.append(pltpu.make_async_copy(parts[i], hold_ref.at[i], in_sems.at[i]))
        to = out_ref.at[:, share, :, pl.ds(pl.multiple_of(source(me_ref[0]) * cap, cap), cap)]
        stores.append(pltpu.make_async_copy(hold_ref.at[i], to, out_sems.at[i]))
    for load in loads:
        load.start()
    for load, store in zip(loads, stores):
        load.wait()
        store.start()
    for store in stores:
        store.wait()


def join(shares, me, parts, whole, total, slices):
    count = len(parts)
    rows, cap = parts[0].shape
    narrow = rows // slices
    parts = [part.reshape(slices, narrow, cap) for part in parts]
    kept = () if whole is None else (whole,)
    return pl.pallas_call(
        functools.partial(join_body, shares),
        in_specs=[SMEM] + [ANY] * count + [HBM] * len(kept),
        out_specs=HBM,
        out_shape=jax.ShapeDtypeStruct((slices, SHARES, narrow, total * cap), f32),
        scratch_shapes=[
            pltpu.VMEM((count, slices, narrow, cap), f32),
            pltpu.SemaphoreType.DMA((count,)),
            pltpu.SemaphoreType.DMA((count,)),
        ],
        input_output_aliases={1 + count: 0} if kept else {},
        compiler_params=params(JOIN),
        cost_estimate=pl.CostEstimate(flops=0, bytes_accessed=count << 19, transcendentals=0),
        name="join",
    )(me, *parts, *kept)


def exchange(picked, step, tgt):
    count = lax.axis_size("row")
    chips, cores = count // 2, 2
    me = lax.axis_index("row").astype(i32)[None]
    slices = lax.axis_size("col")

    def toward(dy, dc, of):
        y, core = of // cores, of % cores
        return (y + dy) % chips * cores + (core + dc) % cores

    def send(part, dy, dc):
        if (dy, dc) == (0, 0):
            return part
        return lax.ppermute(part, "row", [(s, toward(dy, dc, s)) for s in range(count)])

    near = [(1, 0), (chips - 1, 0), (1, 1), (chips - 1, 1)]
    far = [(dy, dc) for dy in range(2, chips - 1) for dc in range(2)]
    own = [(0, 1), (0, 0)]
    shifts = far + near + own
    towards = [functools.partial(toward, dy, dc) for dy, dc in shifts]
    sources = [functools.partial(toward, chips - dy, cores - dc) for dy, dc in shifts]
    first, *later = picked
    later, step = lax.optimization_barrier((later, step))
    got, made = {}, [tgt]
    for h, part in enumerate([first, *later]):
        old = lax.all_to_all(part, "col", 0, 0, tiled=True)
        made = list(place(h, towards, me, old, step, tgt, made[0]))
        for i, part in enumerate(made):
            got[h, i] = send(part, *shifts[i])
    groups = []
    for h in range(SHARES):
        first = [(h, i) for i in range(len(far))]
        later = [(h, len(far) + i) for i in range(len(near))]
        mine = [(h, len(near) + len(far) + i) for i in range(len(own))]
        if h == SHARES - 1:
            groups += [first + mine, later[:2], later[2:]]
        else:
            groups += [first + mine, later]
    whole = None
    for group in groups:
        shares = tuple((h, sources[i]) for h, i in group)
        whole = join(shares, me, [got[key] for key in group], whole, count, slices)
    return whole.reshape(-1, count * CAP)


def local(table, accum, grad_pooled, bag_of, slots, dirty_rows, owner):
    width_slice, bags = grad_pooled.shape
    col_count = lax.axis_size("col")
    col = lax.axis_index("col")
    n = dirty_rows.shape[1] // col_count
    grad = lax.all_gather(grad_pooled, "col", axis=0, tiled=True)
    tgt, accum_old = plan(col, dirty_rows, owner.T, accum, col_count)
    count = pair_counts(bag_of, slots, col, bags, n)
    picked = gather_rows(table, dirty_rows, col_count, count)
    step, accum_new = steps_of(grad, count, accum_old)
    owned = exchange(picked, step, tgt)
    return owned, accum_new[0]


def solution(mesh):
    return jax.shard_map(
        local,
        mesh=mesh,
        in_specs=(
            P("col", "row"),
            P("row"),
            P("col", "row"),
            P("row", None),
            P("row", None),
            P("row", None),
            P("row", None),
        ),
        out_specs=(P(None, ("row", "col")), P(("row", "col"))),
        check_vma=False,
    )
```

```python
import functools

import jax
import jax.numpy as jnp
from jax import lax
from jax.experimental import pallas as pl
from jax.experimental.pallas import tpu as pltpu
from jax.sharding import PartitionSpec as P

learn_rate = 0.3
epsilon = 1e-08

LANES = 128
CAP = 256
CHUNK = 512
BAGS = 64
PAIRS = 5
LOW = 256
WHOLE = 60
JOIN = 4
SHARES = 2

f32, bf16, i32 = jnp.float32, jnp.bfloat16, jnp.int32
NT = (((1,), (1,)), ((), ()))
NN = (((1,), (0,)), ((), ()))


def split(x):
    high = x.astype(bf16)
    return high, (x - high.astype(f32)).astype(bf16)


def params(mib):
    return pltpu.CompilerParams(vmem_limit_bytes=mib * 1024 * 1024)


SMEM = pl.BlockSpec(memory_space=pltpu.SMEM)
VMEM = pl.BlockSpec(memory_space=pltpu.VMEM)
ANY = pl.BlockSpec(memory_space=pl.ANY)
HBM = pl.BlockSpec(memory_space=pltpu.HBM)


def plan_body(col_ref, row_ref, own_ref, accum_ref, tgt_ref, acc_ref):
    n = row_ref.shape[1]
    row, own = row_ref[...], own_ref[...]
    named = jnp.where(lax.broadcasted_iota(i32, (8, n), 0) == own, 1.0, 0.0)
    earlier = lax.broadcasted_iota(i32, (n, n), 0) < lax.broadcasted_iota(i32, (n, n), 1)
    earlier = jnp.where(earlier, 1.0, 0.0).astype(bf16)
    before = lax.dot_general(named.astype(bf16), earlier, NN, preferred_element_type=f32)
    place = jnp.sum(named * before, axis=0, keepdims=True).astype(i32)
    tgt_ref[...] = own * CAP + place
    tall = accum_ref.shape[0]
    picker = jnp.where(
        lax.broadcasted_iota(i32, (tall, n), 0) == row // LANES, 1.0, 0.0
    )
    wide = lax.dot_general(
        accum_ref[...].T, picker, NN, precision=lax.Precision.HIGHEST, preferred_element_type=f32
    )
    keep = lax.broadcasted_iota(i32, (LANES, n), 0) == row % LANES
    acc_ref[...] = jnp.sum(jnp.where(keep, wide, 0.0), axis=0, keepdims=True)


def plan(col, rows, owners, accum, blocks):
    assert blocks % 8 == 0
    n = rows.shape[1] // blocks
    accum = accum.reshape(-1, LANES)
    own = lambda i, c: (0, c[0])
    return pl.pallas_call(
        plan_body,
        grid_spec=pltpu.PrefetchScalarGridSpec(
            num_scalar_prefetch=1,
            grid=(1,),
            in_specs=[
                pl.BlockSpec((1, n), own),
                pl.BlockSpec((1, n), own),
                pl.BlockSpec(accum.shape, lambda i, c: (0, 0)),
            ],
            out_specs=[pl.BlockSpec((1, n), lambda i, c: (0, 0))] * 2,
        ),
        out_shape=(jax.ShapeDtypeStruct((1, n), i32), jax.ShapeDtypeStruct((1, n), f32)),
        compiler_params=params(16),
        name="plan",
    )(col[None], rows, owners, accum)


def counts_body(block_ref, end_ref, bag_ref, slot_ref, out_ref):
    highs, bags, low = out_ref.shape
    span = highs * low
    rows = highs * BAGS
    chunks = bag_ref.shape[1] // CHUNK
    pairs = chunks + bags // BAGS - 1
    assert pairs % PAIRS == 0

    def clear(i, carry):
        for h in range(highs):
            out_ref[h, pl.ds(pl.multiple_of(i * BAGS, BAGS), BAGS), :] = jnp.zeros(
                (BAGS, low), bf16
            )
        return carry

    lax.fori_loop(0, bags // BAGS, clear, 0)
    start = block_ref[0] * span
    left_iota = lax.broadcasted_iota(i32, (rows, CHUNK), 0).astype(f32).astype(bf16)
    right_iota = lax.broadcasted_iota(i32, (low, CHUNK), 0).astype(f32).astype(bf16)
    one, zero = jnp.ones((), bf16), jnp.zeros((), bf16)

    def some(j, carry):
        i, w = carry
        done = []
        for u in range(PAIRS):
            at = pl.ds(pl.multiple_of(i * CHUNK, CHUNK), CHUNK)
            slot = slot_ref[:, at] - start
            near = bag_ref[:, at] - w * BAGS
            inside = (slot >= 0) & (slot < span) & (near >= 0) & (near < BAGS)
            left_id = jnp.where(inside, (slot // low) * BAGS + near, -1)
            left_id = left_id.astype(f32).astype(bf16)
            right_id = (slot & (low - 1)).astype(f32).astype(bf16)
            left = jnp.where(left_iota == left_id, one, zero)
            right = jnp.where(right_iota == right_id, one, zero)
            done.append((w, lax.dot_general(left, right, NT, preferred_element_type=f32)))
            more = w < end_ref[0, i * CHUNK + CHUNK - 1] // BAGS
            i, w = (
                jnp.where(more, i, jnp.minimum(i + 1, chunks - 1)),
                jnp.where(more, w + 1, w),
            )
        for v, both in done:
            at = pl.ds(pl.multiple_of(v * BAGS, BAGS), BAGS)
            for h in range(highs):
                piece = both[h * BAGS : (h + 1) * BAGS].astype(bf16)
                out_ref[h, at, :] = out_ref[h, at, :] + piece
        return i, w

    lax.fori_loop(0, pairs // PAIRS, some, (0, 0))


def pair_counts(bag_of, slots, block, bags, span):
    smem = pl.BlockSpec(memory_space=pltpu.SMEM)
    vmem = pl.BlockSpec(memory_space=pltpu.VMEM)
    return pl.pallas_call(
        counts_body,
        out_shape=jax.ShapeDtypeStruct((span // LOW, bags, LOW), bf16),
        in_specs=[smem, smem, vmem, vmem],
        out_specs=vmem,
        compiler_params=params(12),
        cost_estimate=pl.CostEstimate(flops=int(8e9), bytes_accessed=5 << 20, transcendentals=0),
        name="pair_counts",
    )(block[None], bag_of, bag_of, slots)


def gather_body(row_ref, part_ref, table_ref, after_ref, *refs):
    out_refs, (tall_ref, stage_ref) = refs[:SHARES], refs[SHARES:]
    width, columns = table_ref.shape
    parts = LANES // width
    height = columns // parts
    blocks, narrow, n = out_refs[0].shape
    per = n // LANES
    tiles = blocks * per

    def turn(i, carry):
        at = pl.multiple_of(i * LANES, LANES)
        wide = [table_ref[:, pl.ds(pl.multiple_of(q * height + at, LANES), LANES)] for q in range(parts)]
        tall_ref[pl.ds(at, LANES), :] = jnp.concatenate(wide, axis=0).T
        return carry

    lax.fori_loop(0, height // LANES, turn, 0, unroll=2)

    def fetch(t, slot):
        for u in range(LANES):
            row = row_ref[0, t * LANES + u] & (height - 1)
            stage_ref[slot, u : u + 1, :] = tall_ref[pl.ds(row, 1), :]

    def emit(t, slot):
        flat = stage_ref[slot].T
        part = part_ref[:, pl.ds(pl.multiple_of(t * LANES, LANES), LANES)] // height
        picked = flat[:width]
        for q in range(1, parts):
            picked = jnp.where(part == q, flat[q * width : (q + 1) * width], picked)
        at = pl.ds(pl.multiple_of((t % per) * LANES, LANES), LANES)
        for h, out_ref in enumerate(out_refs):
            out_ref[t // per, :, at] = picked[h * narrow : (h + 1) * narrow]

    fetch(0, 0)

    def two(i, carry):
        fetch(2 * i + 1, 1)
        emit(2 * i, 0)
        fetch(jnp.minimum(2 * i + 2, tiles - 1), 0)
        emit(2 * i + 1, 1)
        return carry

    lax.fori_loop(0, tiles // 2, two, 0)


def gather_rows(table, rows, blocks, after):
    width, columns = table.shape
    n = rows.shape[1] // blocks
    return pl.pallas_call(
        gather_body,
        in_specs=[SMEM, VMEM, VMEM, ANY],
        out_specs=[VMEM] * SHARES,
        out_shape=(jax.ShapeDtypeStruct((blocks, width // SHARES, n), f32),) * SHARES,
        scratch_shapes=[
            pltpu.VMEM((columns * width // LANES, LANES), f32),
            pltpu.VMEM((2, LANES, LANES), f32),
        ],
        compiler_params=params(24),
        cost_estimate=pl.CostEstimate(flops=int(1e9), bytes_accessed=10 << 20, transcendentals=0),
        name="gather_rows",
    )(rows, rows, table, after)


def step_body(grad_ref, count_ref, old_ref, step_ref, new_ref, *scratch):
    wide_ref, both_ref, hold_ref, out_ref, grad_sems, count_sems, out_sems = scratch
    width, bags = grad_ref.shape
    highs, _, low = count_ref.shape
    cuts = grad_sems.shape[0]
    deep = width // cuts
    assert both_ref.shape == (cuts, 2 * deep, bags)
    grads = [
        pltpu.make_async_copy(
            grad_ref.at[i * deep : (i + 1) * deep, :],
            wide_ref.at[i * deep : (i + 1) * deep, :],
            grad_sems.at[i],
        )
        for i in range(cuts)
    ]
    counts = [
        pltpu.make_async_copy(count_ref.at[h], hold_ref.at[h], count_sems.at[h])
        for h in range(highs)
    ]
    outs = [
        pltpu.make_async_copy(
            out_ref.at[h], step_ref.at[:, h * low : (h + 1) * low], out_sems.at[h]
        )
        for h in range(highs)
    ]
    for copy in (*grads, counts[0]):
        copy.start()
    for i in range(cuts):
        grads[i].wait()
        if i == cuts - 1:
            for copy in counts[1:]:
                copy.start()

        def cut(j, carry):
            high, low = split(wide_ref[pl.ds(pl.multiple_of(i * deep + j * 32, 32), 32), :])
            both_ref[i, pl.ds(pl.multiple_of(j * 32, 32), 32), :] = high
            both_ref[i, pl.ds(pl.multiple_of(deep + j * 32, 32), 32), :] = low
            return carry

        lax.fori_loop(0, deep // 32, cut, 0)

    for h in range(highs):
        counts[h].wait()

        def one(i, total):
            got = lax.dot_general(both_ref[i], hold_ref[h], NN, preferred_element_type=f32)
            got = got[:deep] + got[deep:]
            out_ref[h, pl.ds(pl.multiple_of(i * deep, deep), deep), :] = got
            return total + jnp.sum(got * got, axis=0, keepdims=True)

        total = lax.fori_loop(0, cuts, one, jnp.zeros((1, low), f32))
        here = slice(h * low, (h + 1) * low)
        new = old_ref[:, here] + total / width
        new_ref[:, here] = new
        out_ref[h] = out_ref[h] * (learn_rate / (jnp.sqrt(new) + epsilon))
        outs[h].start()
    for copy in outs:
        copy.wait()


def steps_of(grad, count, old):
    width, bags = grad.shape
    highs, _, low = count.shape
    cuts = 2
    return pl.pallas_call(
        step_body,
        in_specs=[HBM, HBM, VMEM],
        out_specs=[HBM, VMEM],
        out_shape=(
            jax.ShapeDtypeStruct((width, highs * low), f32),
            jax.ShapeDtypeStruct((1, highs * low), f32),
        ),
        scratch_shapes=[
            pltpu.VMEM((width, bags), f32),
            pltpu.VMEM((cuts, 2 * width // cuts, bags), bf16),
            pltpu.VMEM(count.shape, bf16),
            pltpu.VMEM((highs, width, low), f32),
            pltpu.SemaphoreType.DMA((cuts,)),
            pltpu.SemaphoreType.DMA((highs,)),
            pltpu.SemaphoreType.DMA((highs,)),
        ],
        compiler_params=params(WHOLE),
        cost_estimate=pl.CostEstimate(flops=int(8e9), bytes_accessed=10 << 20, transcendentals=0),
        name="steps_of",
    )(grad, count, old)


def place_body(share, towards, me_ref, old_ref, step_ref, tgt_ref, after_ref, *refs):
    out_refs, scratch = refs[:-6], refs[-6:]
    old_hold, step_hold, both_ref, hold_ref, loads, sems = scratch
    slices, narrow, n = old_ref.shape
    rows = slices * narrow
    tgt = tgt_ref[...]
    chunks = loads.shape[0]
    deep = slices // chunks
    waits = []
    for i in range(chunks):
        at = slice(i * deep, (i + 1) * deep)
        waits.append(
            (
                pltpu.make_async_copy(old_ref.at[at], old_hold.at[at], loads.at[i, 0]),
                pltpu.make_async_copy(step_ref.at[at, share], step_hold.at[at], loads.at[i, 1]),
            )
        )
        for copy in waits[-1]:
            copy.start()

    def cut(f, carry):
        high, low = split(old_hold[f] - step_hold[f])
        both_ref[pl.ds(pl.multiple_of(f * narrow, narrow), narrow), :] = high
        both_ref[pl.ds(pl.multiple_of(rows + f * narrow, narrow), narrow), :] = low
        return carry

    for i in range(chunks):
        for copy in waits[i]:
            copy.wait()
        lax.fori_loop(i * deep, (i + 1) * deep, cut, 0, unroll=True)
    slot = lax.broadcasted_iota(i32, (CAP, n), 0)
    copies = []
    for i, out_ref in enumerate(out_refs):
        here = jnp.where(slot == tgt - towards[i](me_ref[0]) * CAP, 1.0, 0.0).astype(bf16)
        total = lax.dot_general(both_ref[...], here, NT, preferred_element_type=f32)
        hold_ref[i] = total[:rows] + total[rows:]
        copies.append(pltpu.make_async_copy(hold_ref.at[i], out_ref, sems.at[i]))
        copies[-1].start()
    for copy in copies:
        copy.wait()


def place(share, towards, me, old, step, tgt, after):
    count = len(towards)
    rows = old.shape[0] * old.shape[1]
    return pl.pallas_call(
        functools.partial(place_body, share, towards),
        in_specs=[SMEM, HBM, HBM, VMEM, ANY],
        out_specs=[HBM] * count,
        out_shape=(jax.ShapeDtypeStruct((rows, CAP), f32),) * count,
        scratch_shapes=[
            pltpu.VMEM(old.shape, f32),
            pltpu.VMEM(old.shape, f32),
            pltpu.VMEM((2 * rows, old.shape[2]), bf16),
            pltpu.VMEM((count, rows, CAP), f32),
            pltpu.SemaphoreType.DMA((4, 2)),
            pltpu.SemaphoreType.DMA((count,)),
        ],
        compiler_params=params(WHOLE),
        cost_estimate=pl.CostEstimate(flops=int(2e9), bytes_accessed=6 << 20, transcendentals=0),
        name="place",
    )(me, old, step.reshape(old.shape[0], SHARES, *old.shape[1:]), tgt, after)


def join_body(shares, me_ref, *refs):
    count = len(shares)
    parts, (out_ref, hold_ref, in_sems, out_sems) = refs[:count], refs[-4:]
    cap = hold_ref.shape[3]
    loads, stores = [], []
    for i, (share, source) in enumerate(shares):
        loads.append(pltpu.make_async_copy(parts[i], hold_ref.at[i], in_sems.at[i]))
        to = out_ref.at[:, share, :, pl.ds(pl.multiple_of(source(me_ref[0]) * cap, cap), cap)]
        stores.append(pltpu.make_async_copy(hold_ref.at[i], to, out_sems.at[i]))
    for load in loads:
        load.start()
    for load, store in zip(loads, stores):
        load.wait()
        store.start()
    for store in stores:
        store.wait()


def join(shares, me, parts, whole, total, slices):
    count = len(parts)
    rows, cap = parts[0].shape
    narrow = rows // slices
    parts = [part.reshape(slices, narrow, cap) for part in parts]
    kept = () if whole is None else (whole,)
    return pl.pallas_call(
        functools.partial(join_body, shares),
        in_specs=[SMEM] + [ANY] * count + [HBM] * len(kept),
        out_specs=HBM,
        out_shape=jax.ShapeDtypeStruct((slices, SHARES, narrow, total * cap), f32),
        scratch_shapes=[
            pltpu.VMEM((count, slices, narrow, cap), f32),
            pltpu.SemaphoreType.DMA((count,)),
            pltpu.SemaphoreType.DMA((count,)),
        ],
        input_output_aliases={1 + count: 0} if kept else {},
        compiler_params=params(JOIN),
        cost_estimate=pl.CostEstimate(flops=0, bytes_accessed=count << 19, transcendentals=0),
        name="join",
    )(me, *parts, *kept)


def exchange(picked, step, tgt):
    count = lax.axis_size("row")
    chips, cores = count // 2, 2
    me = lax.axis_index("row").astype(i32)[None]
    slices = lax.axis_size("col")

    def toward(dy, dc, of):
        y, core = of // cores, of % cores
        return (y + dy) % chips * cores + (core + dc) % cores

    def send(part, dy, dc):
        if (dy, dc) == (0, 0):
            return part
        return lax.ppermute(part, "row", [(s, toward(dy, dc, s)) for s in range(count)])

    near = [(1, 0), (chips - 1, 0), (1, 1), (chips - 1, 1)]
    far = [(dy, dc) for dy in range(2, chips - 1) for dc in range(2)]
    own = [(0, 1), (0, 0)]
    shifts = far + near + own
    towards = [functools.partial(toward, dy, dc) for dy, dc in shifts]
    sources = [functools.partial(toward, chips - dy, cores - dc) for dy, dc in shifts]
    first, *later = picked
    later, step = lax.optimization_barrier((later, step))
    got, made = {}, [tgt]
    for h, part in enumerate([first, *later]):
        old = lax.all_to_all(part, "col", 0, 0, tiled=True)
        made = list(place(h, towards, me, old, step, tgt, made[0]))
        for i, part in enumerate(made):
            got[h, i] = send(part, *shifts[i])
    groups = []
    for h in range(SHARES):
        first = [(h, i) for i in range(len(far))]
        later = [(h, len(far) + i) for i in range(len(near))]
        mine = [(h, len(near) + len(far) + i) for i in range(len(own))]
        if h == SHARES - 1:
            groups += [first + mine, later[:2], later[2:]]
        else:
            groups += [first + mine, later]
    whole = None
    for group in groups:
        shares = tuple((h, sources[i]) for h, i in group)
        whole = join(shares, me, [got[key] for key in group], whole, count, slices)
    return whole.reshape(-1, count * CAP)


def local(table, accum, grad_pooled, bag_of, slots, dirty_rows, owner):
    width_slice, bags = grad_pooled.shape
    col_count = lax.axis_size("col")
    col = lax.axis_index("col")
    n = dirty_rows.shape[1] // col_count
    grad = lax.all_gather(grad_pooled, "col", axis=0, tiled=True)
    tgt, accum_old = plan(col, dirty_rows, owner.T, accum, col_count)
    count = pair_counts(bag_of, slots, col, bags, n)
    picked = gather_rows(table, dirty_rows, col_count, count)
    step, accum_new = steps_of(grad, count, accum_old)
    owned = exchange(picked, step, tgt)
    return owned, accum_new[0]


def solution(mesh):
    return jax.shard_map(
        local,
        mesh=mesh,
        in_specs=(
            P("col", "row"),
            P("row"),
            P("col", "row"),
            P("row", None),
            P("row", None),
            P("row", None),
            P("row", None),
        ),
        out_specs=(P(None, ("row", "col")), P(("row", "col"))),
        check_vma=False,
    )
```
